256 devices in a mesh: seq: 16 (over y, x_lo, core), tp: 16 (over x_hi, z).
Axes of the slice: x: 4 (x_hi: 2, x_lo: 2; x = x_hi * 2 + x_lo), y: 4, z: 8, core: 2. Of those that a mesh axis runs over, the one named last changes fastest.
Arguments:
- tokens: bfloat16 [6144, 4096], P('seq'), may hold values from -14 to 14
- w_query: bfloat16 [4096, 4096], P(None, 'tp'), may hold values from -0.09375 to 0.09375
- w_key: bfloat16 [4096, 4096], P(None, 'tp'), may hold values from -0.09375 to 0.09375
- w_value: bfloat16 [4096, 4096], P(None, 'tp'), may hold values from -0.09375 to 0.09375
- grad_out: bfloat16 [6144, 4096], P('seq', 'tp'), may hold values from -6 to 6
Outputs:
- grad_tokens: bfloat16 [6144, 4096], P('seq')
The draws below stay inside these ranges and needn't reach their ends.
All inputs are finite; a program needn't handle non-finite values.
Results may differ from the reference program's by a relative error of at most 0.03.
Values may be sent and summed in bfloat16 or wider, within the bound.
A program may use at most 128 MiB of HBM per device.

```python
import jax
import jax.numpy as jnp
from jax import lax

D = 4096
HEADS = 32
HEAD = 128
TOK_DEV = 384
TOKENS = 6144
N_SEQ = 16


def draw_tokens(key, part):
    key = jax.random.fold_in(key, 7)
    base_key = jax.random.fold_in(key, 0)
    values = jax.random.truncated_normal(base_key, -6.0, 6.0, (TOKENS, D), jnp.float32)
    return values.astype(jnp.bfloat16)


def shard_levels(own_key, shape, cuts, smallest, top_value):
    def one(axis_at, parts):
        draws = jax.random.uniform(jax.random.fold_in(jax.random.fold_in(own_key, 6), axis_at), (parts,), jnp.float32, smallest / len(cuts), top_value / len(cuts))
        return jnp.repeat(jnp.exp(draws), shape[axis_at] // parts).reshape((-1,) + (1,) * (len(shape) - axis_at - 1))

    factor_of = one(*cuts[0])
    for cut in cuts[1:]:
        factor_of = factor_of * one(*cut)
    return factor_of


def scatter_about(rng, shape, spread, reach, cuts=(), kind=jnp.bfloat16):
    entries = spread * jax.random.normal(rng, shape, jnp.float32)
    if cuts:
        entries = entries * shard_levels(rng, shape, cuts, -0.22, 0.18)
    return jnp.clip(entries, -reach, reach).astype(kind)


def setup_inputs(seed: int = 0) -> dict:
    streams_of = jax.random.split(jax.random.key(seed), 6)
    return {
        "tokens": draw_tokens(jax.random.fold_in(streams_of[5], 71), 0),
        "w_query": scatter_about(streams_of[1], (D, HEADS * HEAD), D ** -0.5, 0.09375, ((1, 16),)),
        "w_key": scatter_about(streams_of[2], (D, HEADS * HEAD), D ** -0.5, 0.09375, ((1, 16),)),
        "w_value": scatter_about(streams_of[3], (D, HEADS * HEAD), D ** -0.5, 0.09375, ((1, 16),)),
        "grad_out": scatter_about(streams_of[4], (TOKENS, HEADS * HEAD), 1.0, 6.0, ((0, 16), (1, 16))),
    }


def reference(tokens, w_query, w_key, w_value, grad_out):
    score_scale = HEAD ** -0.5
    queries = jnp.dot(tokens, w_query, preferred_element_type=jnp.float32).astype(jnp.bfloat16)
    keys_all = jnp.dot(tokens, w_key, preferred_element_type=jnp.float32).astype(jnp.bfloat16)
    values_all = jnp.dot(tokens, w_value, preferred_element_type=jnp.float32).astype(jnp.bfloat16)
    positions = jnp.arange(TOKENS, dtype=jnp.int32)
    times = (positions % TOK_DEV) * N_SEQ + positions // TOK_DEV
    allowed = times[None, :] <= times[:, None]

    def one_head(head):
        start = (head * HEAD).astype(jnp.int32)
        query_h = lax.dynamic_slice_in_dim(queries, start, HEAD, 1)
        key_h = lax.dynamic_slice_in_dim(keys_all, start, HEAD, 1)
        value_h = lax.dynamic_slice_in_dim(values_all, start, HEAD, 1)
        grad_h = lax.dynamic_slice_in_dim(grad_out, start, HEAD, 1)
        scores = jnp.dot(query_h, key_h.T, preferred_element_type=jnp.float32) * score_scale
        scores = jnp.where(allowed, scores, -1e30)
        top = jnp.max(scores, axis=1, keepdims=True)
        weights = jnp.exp(scores - top)
        total = jnp.sum(weights, axis=1, keepdims=True)
        logsum = top + jnp.log(total)
        attended = (jnp.dot(weights.astype(jnp.bfloat16), value_h, preferred_element_type=jnp.float32) / total).astype(jnp.bfloat16)
        row_delta = jnp.sum(grad_h.astype(jnp.float32) * attended.astype(jnp.float32), axis=1, keepdims=True)
        probs = jnp.exp(scores - logsum)
        grad_value = jnp.dot(probs.astype(jnp.bfloat16).T, grad_h, preferred_element_type=jnp.float32)
        grad_probs = jnp.dot(grad_h, value_h.T, preferred_element_type=jnp.float32)
        grad_scores = (probs * (grad_probs - row_delta)).astype(jnp.bfloat16)
        grad_query = jnp.dot(grad_scores, key_h, preferred_element_type=jnp.float32) * score_scale
        grad_key = jnp.dot(grad_scores.T, query_h, preferred_element_type=jnp.float32) * score_scale
        return grad_query, grad_key, grad_value

    grad_query, grad_key, grad_value = lax.map(one_head, jnp.arange(HEADS, dtype=jnp.int32))

    def merge_heads(stacked):
        return jnp.transpose(stacked, (1, 0, 2)).reshape(TOKENS, HEADS * HEAD).astype(jnp.bfloat16)

    partial_sum = jnp.dot(merge_heads(grad_query), w_query.T, preferred_element_type=jnp.float32)
    partial_sum = partial_sum + jnp.dot(merge_heads(grad_key), w_key.T, preferred_element_type=jnp.float32)
    partial_sum = partial_sum + jnp.dot(merge_heads(grad_value), w_value.T, preferred_element_type=jnp.float32)
    return partial_sum.astype(jnp.bfloat16)
```

```python
import functools

import jax
import jax.numpy as jnp
from jax import lax
from jax.experimental import pallas as pl
from jax.experimental.pallas import tpu as pltpu
from jax.sharding import PartitionSpec as P

MESH = pl.DeviceIdType.MESH
HEAD = 128
ROWS = 384
D = 4096
SUB = 3
F32 = jnp.float32
BF16 = jnp.bfloat16
LOG2E = 1.4426950408889634
SCALE = HEAD ** (-0.5)
NEG = -1e30
FLOOR = -1e29
COPIES = 160
LOCALS = 48
HALF = ROWS // 2


def nt(a, b):
    return lax.dot_general(a, b, (((1,), (1,)), ((), ())), preferred_element_type=F32)


def nn(a, b):
    return jnp.dot(a, b, preferred_element_type=F32)


def kernel(
    tok, wq, wk, wv, do, out,
    tok_v, wq_v, wk_v, wv_v,
    q_own, k_own, v_own,
    q_all, do_all, k_all, v_all, k_t,
    key_time, w_s, dp_s, stat, row_tx, row_rx, row_all,
    p_buf, ds_buf, dk_acc, dv_acc,
    dq_tx, dkv_tx, dq_rx, dkv_rx, grads,
    x_tx, x_rx, b_tx, b_rx, a_tx, a_rx, swap_tx, swap_rx, out_b, out_a,
    send_sem, recv_sem, local_sem,
):
    s = lax.axis_index("seq")
    t = lax.axis_index("tp")
    y, xl, c = s // 4, lax.rem(s // 2, 2), lax.rem(s, 2)
    xh, z = t // 8, lax.rem(t, 8)

    def dev(dy=0, dx=0, dc=0, dh=0, dz=0):
        seq = lax.rem(y + dy, 4) * 4 + lax.rem(xl + dx, 2) * 2 + lax.rem(c + dc, 2)
        return (seq, lax.rem(xh + dh, 2) * 8 + lax.rem(z + dz + 8, 8))

    started = []
    counts = [0, 0]

    def send(src, dst, to):
        i = counts[0]
        counts[0] += 1
        copy = pltpu.make_async_remote_copy(
            src_ref=src, dst_ref=dst, send_sem=send_sem.at[i], recv_sem=recv_sem.at[i],
            device_id=to, device_id_type=MESH,
        )
        copy.start()
        started.append(copy)
        return copy

    def local(src, dst):
        i = counts[1]
        counts[1] += 1
        copy = pltpu.make_async_copy(src, dst, local_sem.at[i])
        copy.start()
        return copy

    load_tok = local(tok, tok_v)
    load_k = local(wk, wk_v)
    load_v = local(wv, wv_v)
    load_q = local(wq, wq_v)

    barrier = pltpu.get_barrier_semaphore()
    partners = [dev(dy=dy, dc=dc) for dy in range(4) for dc in range(2) if dy or dc]
    partners += [dev(dx=1, dc=dc) for dc in range(2)]
    partners += [dev(dz=1), dev(dz=-1), dev(dh=1)]
    for partner in partners:
        pl.semaphore_signal(barrier, inc=1, device_id=partner, device_id_type=MESH)
    pl.semaphore_wait(barrier, len(partners))

    def other(e):
        return lax.rem(c + e, 2)

    def query_rows(dy):
        return pl.ds(pl.multiple_of(((4 - dy) % 4) * 256 + c * 128, 128), 128)

    key_rows = pl.ds(pl.multiple_of((xl * 2 + c) * 128, 128), 128)
    order = [(0, 1), (1, 0), (1, 1), (3, 0), (3, 1), (2, 0), (2, 1)]

    def head_lanes(e):
        return pl.ds(pl.multiple_of(other(e) * 128, 128), 128)

    got_do = {(0, 0): local(do.at[:, :, head_lanes(0)], do_all.at[:, query_rows(0), :])}
    for dy, e in order:
        got_do[dy, e] = send(
            do.at[:, :, head_lanes(e)], do_all.at[:, query_rows(dy), :], dev(dy=dy, dc=e)
        )

    def project(weight, own):
        product = nn(tok_v[...], weight[...]).astype(BF16)
        for h in range(2):
            for a in range(SUB):
                own[h, a] = product[a * 128 : (a + 1) * 128, h * 128 : (h + 1) * 128]

    def share_keys(own, everyone):
        copies = [local(own.at[c], everyone.at[:, key_rows, :])]
        for dx, e in ((1, 0), (1, 1), (0, 1)):
            copies.append(send(own.at[other(e)], everyone.at[:, key_rows, :], dev(dx=dx, dc=e)))
        return copies

    load_tok.wait()
    load_k.wait()
    project(wk_v, k_own)
    got_k = share_keys(k_own, k_all)
    load_v.wait()
    project(wv_v, v_own)
    got_v = share_keys(v_own, v_all)
    load_q.wait()
    project(wq_v, q_own)
    got_q = {(0, 0): local(q_own.at[c], q_all.at[:, query_rows(0), :])}
    for dy, e in order:
        got_q[dy, e] = send(q_own.at[other(e)], q_all.at[:, query_rows(dy), :], dev(dy=dy, dc=e))

    row = lax.broadcasted_iota(jnp.int32, (512, 256), 0)
    key_time[...] = (row & 127) * 16 + y * 4 + (row >> 7)

    def arrived(copies):
        copies[0].wait()
        for copy in copies[1:]:
            copy.wait_recv()

    arrived(got_k)
    for a in range(SUB):
        k_t[a] = k_all[a].T
    arrived(got_v)

    exponent = SCALE * LOG2E
    for dq in (0, 3, 1, 2):
        dy = (4 - dq) % 4
        for e in range(2):
            if dy == 0 and e == 0:
                got_q[dy, e].wait()
                got_do[dy, e].wait()
            else:
                got_q[dy, e].wait_recv()
                got_do[dy, e].wait_recv()
        lanes = slice(dq * 256, (dq + 1) * 256)
        col = lax.broadcasted_iota(jnp.int32, (1, 256), 1)
        query_time = (col & 127) * 16 + lax.rem(y + dq, 4) * 4 + xl * 2 + (col >> 7)

        def tile(a, j, slot, masked, lanes=lanes, query_time=query_time):
            scores = nt(k_all[j], q_all[a, lanes, :])
            if masked:
                scores = jnp.where(key_time[...] <= query_time, scores, NEG)
            top = jnp.maximum(jnp.max(scores, axis=0, keepdims=True), FLOOR)
            weights = jnp.exp2((scores - top) * exponent)
            grad_probs = nt(v_all[j], do_all[a, lanes, :])
            stat[slot, 0:1, lanes] = top
            stat[slot, 1:2, lanes] = jnp.sum(weights, axis=0, keepdims=True)
            stat[slot, 2:3, lanes] = jnp.sum(weights * grad_probs, axis=0, keepdims=True)
            w_s[slot, :, lanes] = weights.astype(BF16)
            dp_s[slot, :, lanes] = grad_probs.astype(BF16)

        @pl.loop(0, 3)
        def _(i, tile=tile):
            tile(i, i, i, True)

        @pl.loop(0, 3)
        def _(i, tile=tile):
            tile((i + 3) // 2, i // 2, i + 3, False)

    def slots_of(a):
        return [(j, a if j == a else 2 + a + j) for j in range(a + 1)]

    for a in range(SUB):
        slots = [slot for _, slot in slots_of(a)]
        top = functools.reduce(jnp.maximum, [stat[i, 0:1, :] for i in slots])
        total = jnp.zeros_like(top)
        moment = jnp.zeros_like(top)
        for i in slots:
            factor = jnp.exp2((stat[i, 0:1, :] - top) * exponent)
            total += stat[i, 1:2, :] * factor
            moment += stat[i, 2:3, :] * factor
        some = jnp.maximum(total, 1e-30)
        row_tx[2 * a : 2 * a + 1, :] = top * exponent + jnp.log(some) * LOG2E
        row_tx[2 * a + 1 : 2 * a + 2, :] = moment / some
    row_tx[6:8, :] = jnp.zeros((2, 1024), F32)
    got_rows = {dy: send(row_tx, row_rx.at[3 - dy], dev(dy=dy)) for dy in (1, 3, 2)}
    for dy in (1, 3, 2):
        got_rows[dy].wait_recv()
    for a in range(SUB):
        for dq in range(4):
            lanes = slice(dq * 256, (dq + 1) * 256)
            sums = [row_tx[2 * a : 2 * a + 1, lanes]]
            deltas = [row_tx[2 * a + 1 : 2 * a + 2, lanes]]
            for dy in (1, 2, 3):
                far = ((dq - dy) % 4) * 256
                sums.append(row_rx[dy - 1, 2 * a : 2 * a + 1, far : far + 256])
                deltas.append(row_rx[dy - 1, 2 * a + 1 : 2 * a + 2, far : far + 256])
            top = functools.reduce(jnp.maximum, sums)
            logsum = top + LOG2E * jnp.log(sum(jnp.exp2(v - top) for v in sums))
            row_all[2 * a : 2 * a + 1, lanes] = logsum
            row_all[2 * a + 1 : 2 * a + 2, lanes] = sum(
                d * jnp.exp2(v - logsum) for v, d in zip(sums, deltas)
            )

    got_dq = []
    got_dkv = []
    turn = 0
    for a in (2, 1, 0):
        logsum = row_all[2 * a : 2 * a + 1, :]
        delta = row_all[2 * a + 1 : 2 * a + 2, :]
        grad_q = None
        for j, slot in reversed(slots_of(a)):
            side = turn % 2
            turn += 1
            factor = jnp.exp2(stat[slot, 0:1, :] * exponent - logsum)
            for dq in range(4):
                lanes = slice(dq * 256, (dq + 1) * 256)
                probs = w_s[slot, :, lanes].astype(F32) * factor[:, lanes]
                p_buf[side, :, lanes] = probs.astype(BF16)
                ds_buf[side, :, lanes] = (
                    probs * (dp_s[slot, :, lanes].astype(F32) - delta[:, lanes])
                ).astype(BF16)
            part_v = nn(p_buf[side], do_all[a])
            part_k = nn(ds_buf[side], q_all[a])
            part_q = nn(k_t[j], ds_buf[side])
            grad_q = part_q if grad_q is None else grad_q + part_q
            if a == 2:
                dv_acc[j] = part_v
                dk_acc[j] = part_k
            else:
                dv_acc[j] += part_v
                dk_acc[j] += part_k
        dkv_tx[a, :, 0] = (dk_acc[a] * SCALE).astype(BF16).reshape(4, 128, 128)
        dkv_tx[a, :, 1] = dv_acc[a].astype(BF16).reshape(4, 128, 128)
        dq_tx[a] = (grad_q * SCALE).T.astype(BF16).reshape(4, 2, 128, 128)
        for dx, e in ((1, 0), (1, 1), (0, 1), (0, 0)):
            src = dkv_tx.at[a, lax.rem(xl + dx, 2) * 2 + other(e)]
            dst = dkv_rx.at[a, dx, e]
            if dx or e:
                got_dkv.append(send(src, dst, dev(dx=dx, dc=e)))
            else:
                local(src, dst).wait()
        for dy, e in order[1:] + order[:1] + [(0, 0)]:
            src = dq_tx.at[a, dy, other(e)]
            dst = dq_rx.at[a, (4 - dy) % 4, e]
            if dy or e:
                got_dq.append(send(src, dst, dev(dy=dy, dc=e)))
            else:
                local(src, dst).wait()
    for copy in got_dq + got_dkv:
        copy.wait_recv()
    for a in range(SUB):
        rows = slice(a * 128, (a + 1) * 128)
        for e in range(2):
            base = pl.multiple_of(other(e) * 128, 128)
            total = sum(dq_rx[a, i, e].astype(F32) for i in range(4))
            grads[0, rows, pl.ds(base, 128)] = total.astype(BF16)
            for i in range(2):
                total = dkv_rx[a, 0, e, i].astype(F32) + dkv_rx[a, 1, e, i].astype(F32)
                grads[1 + i, rows, pl.ds(base, 128)] = total.astype(BF16)

    def far(r):
        return lax.rem(z + r + 8, 8)

    def product(start, width):
        rows = pl.ds(pl.multiple_of(start, 128), width)
        return (
            nt(grads[0], wq_v[rows, :]) + nt(grads[1], wk_v[rows, :]) + nt(grads[2], wv_v[rows, :])
        )

    def part_b(r):
        return product(2048 + far(r) * 256, 256)

    def part_a(r, dh):
        return product(lax.rem(xh + dh, 2) * 1024 + far(r) * 128, 128)

    top_rows, low_rows = slice(0, HALF), slice(HALF, ROWS)
    got_x = {}

    def send_x(r):
        x_tx[r + 3] = part_a(r, 1).astype(BF16)
        got_x[r] = send(x_tx.at[r + 3], x_rx.at[r + 3], dev(dh=1))

    got_b = [[None] * 4, [None] * 4]
    got_a = [[None] * 4, [None] * 4]

    def ring_step(step, own, tx, rx, got):
        if step == 0:
            total = own(4).astype(BF16)
            for w, rows in ((0, top_rows), (1, low_rows)):
                tx[w, 0, rows, :] = total[rows]
                got[w][0] = send(
                    tx.at[w, 0, rows, :], rx.at[w, 0, rows, :], dev(dz=1 - 2 * w)
                )
            return
        for w, rows in ((0, top_rows), (1, low_rows)):
            total = own((4 - step) * (1 - 2 * w))
            got[w][step - 1].wait_recv()
            if step == 1:
                tx[w, step] = total.astype(BF16)
                tx[w, step, rows, :] = (total[rows] + rx[w, 0, rows, :].astype(F32)).astype(BF16)
            else:
                tx[w, step] = (total + rx[w, step - 1].astype(F32)).astype(BF16)
            got[w][step] = send(tx.at[w, step], rx.at[w, step], dev(dz=1 - 2 * w))

    def own_a(r):
        term = part_a(r, 0)
        got_x[r].wait_recv()
        return term + x_rx[r + 3].astype(F32)

    send_x(4)
    ring_step(0, part_b, b_tx, b_rx, got_b)
    send_x(3)
    send_x(-3)
    ring_step(1, part_b, b_tx, b_rx, got_b)
    send_x(2)
    send_x(-2)
    ring_step(0, own_a, a_tx, a_rx, got_a)
    send_x(1)
    send_x(-1)
    send_x(0)
    ring_step(2, part_b, b_tx, b_rx, got_b)
    ring_step(1, own_a, a_tx, a_rx, got_a)
    ring_step(3, part_b, b_tx, b_rx, got_b)
    ring_step(2, own_a, a_tx, a_rx, got_a)
    total = part_b(0)
    for w in range(2):
        got_b[w][3].wait_recv()
        total += b_rx[w, 3].astype(F32)
    swap_tx[...] = total.astype(BF16)
    got_swap = send(swap_tx, swap_rx, dev(dh=1))
    ring_step(3, own_a, a_tx, a_rx, got_a)

    stores = []
    gather_b = [[None] * 4, [None] * 4]
    gather_a = [[None] * 4, [None] * 4]
    got_across = {}

    def store_b(r):
        i = far(r)
        lanes = pl.ds(pl.multiple_of(2048 + i * 256, 128), 256)
        stores.append(local(out_b.at[i], out.at[:, lanes]))

    def store_a(r, dh):
        i, h = far(r), lax.rem(xh + dh, 2)
        lanes = pl.ds(pl.multiple_of(h * 1024 + i * 128, 128), 128)
        stores.append(local(out_a.at[h, i], out.at[:, lanes]))

    def pass_on(step, buf, got):
        for w, rows in ((0, top_rows), (1, low_rows)):
            i = far(-step * (1 - 2 * w))
            piece = buf.at[i, rows, :] if step == 3 else buf.at[i]
            got[w][step] = send(piece, piece, dev(dz=1 - 2 * w))

    def across(r):
        i = far(r)
        got_across[r] = send(out_a.at[xh, i], out_a.at[xh, i], dev(dh=1))

    got_swap.wait_recv()
    out_b[z] = (swap_tx[...].astype(F32) + swap_rx[...].astype(F32)).astype(BF16)
    pass_on(0, out_b, gather_b)
    store_b(0)
    total = own_a(0)
    for w in range(2):
        got_a[w][3].wait_recv()
        total += a_rx[w, 3].astype(F32)
    out_a[xh, z] = total.astype(BF16)
    pass_on(0, out_a.at[xh], gather_a)
    across(0)
    store_a(0, 0)
    for step in range(4):
        places = [-step - 1, step + 1] if step < 3 else [4]
        for w in range(2):
            gather_b[w][step].wait_recv()
        if step < 3:
            pass_on(step + 1, out_b, gather_b)
        for r in places:
            store_b(r)
        for w in range(2):
            gather_a[w][step].wait_recv()
        if step < 3:
            pass_on(step + 1, out_a.at[xh], gather_a)
        for r in places:
            across(r)
            store_a(r, 0)
    for r in (0, -1, 1, -2, 2, -3, 3, 4):
        got_across[r].wait_recv()
        store_a(r, 1)
    for copy in stores:
        copy.wait()
    for copy in started:
        copy.wait_send()


def shards(tokens, w_query, w_key, w_value, grad_out):
    anywhere = pl.BlockSpec(memory_space=pl.ANY)
    scratch = [
        ((ROWS, D), BF16), ((D, 256), BF16), ((D, 256), BF16), ((D, 256), BF16),
        ((2, SUB, 128, 128), BF16), ((2, SUB, 128, 128), BF16), ((2, SUB, 128, 128), BF16),
        ((SUB, 1024, 128), BF16), ((SUB, 1024, 128), BF16),
        ((SUB, 512, 128), BF16), ((SUB, 512, 128), BF16), ((SUB, 128, 512), BF16),
        ((512, 256), jnp.int32), ((6, 512, 1024), BF16), ((6, 512, 1024), BF16),
        ((6, 8, 1024), F32), ((8, 1024), F32), ((3, 8, 1024), F32), ((8, 1024), F32),
        ((2, 512, 1024), BF16), ((2, 512, 1024), BF16), ((SUB, 512, 128), F32), ((SUB, 512, 128), F32),
        ((SUB, 4, 2, 128, 128), BF16), ((SUB, 4, 2, 128, 128), BF16),
        ((SUB, 4, 2, 128, 128), BF16), ((SUB, 2, 2, 2, 128, 128), BF16), ((3, ROWS, 256), BF16),
        ((8, ROWS, 128), BF16), ((8, ROWS, 128), BF16),
        ((2, 4, ROWS, 256), BF16), ((2, 4, ROWS, 256), BF16),
        ((2, 4, ROWS, 128), BF16), ((2, 4, ROWS, 128), BF16),
        ((ROWS, 256), BF16), ((ROWS, 256), BF16),
        ((8, ROWS, 256), BF16), ((2, 8, ROWS, 128), BF16),
    ]
    return pl.pallas_call(
        kernel,
        out_shape=jax.ShapeDtypeStruct((ROWS, D), BF16),
        in_specs=[anywhere] * 5,
        out_specs=anywhere,
        scratch_shapes=[pltpu.VMEM(shape, kind) for shape, kind in scratch]
        + [
            pltpu.SemaphoreType.DMA((COPIES,)),
            pltpu.SemaphoreType.DMA((COPIES,)),
            pltpu.SemaphoreType.DMA((LOCALS,)),
        ],
        compiler_params=pltpu.CompilerParams(
            collective_id=0, has_side_effects=True, vmem_limit_bytes=60 * 2**20
        ),
    )(tokens, w_query, w_key, w_value, grad_out.reshape(SUB, 128, 256))


def solution(mesh):
    placed = (P("seq", None), P(None, "tp"), P(None, "tp"), P(None, "tp"), P("seq", "tp"))
    return jax.shard_map(
        shards, mesh=mesh, in_specs=placed, out_specs=P("seq", None), check_vma=False
    )
```

```python
import functools

import jax
import jax.numpy as jnp
from jax import lax
from jax.experimental import pallas as pl
from jax.experimental.pallas import tpu as pltpu
from jax.sharding import PartitionSpec as P

MESH = pl.DeviceIdType.MESH
HEAD = 128
ROWS = 384
D = 4096
SUB = 3
F32 = jnp.float32
BF16 = jnp.bfloat16
LOG2E = 1.4426950408889634
SCALE = HEAD ** (-0.5)
NEG = -1e30
FLOOR = -1e29
COPIES = 200
LOCALS = 48
HALF = ROWS // 2


def nt(a, b):
    return lax.dot_general(a, b, (((1,), (1,)), ((), ())), preferred_element_type=F32)


def nn(a, b):
    return jnp.dot(a, b, preferred_element_type=F32)


def kernel(
    tok, wq, wk, wv, do, out,
    tok_v, wq_v, wk_v, wv_v,
    q_own, k_own, v_own,
    q_all, do_all, k_all, v_all, k_t,
    key_time, w_s, dp_s, tops, totals, moments, row_tx, row_rx, row_all,
    p_buf, ds_buf, dk_acc, dv_acc,
    dq_tx, dkv_tx, dq_rx, dkv_rx, grads,
    x_tx, x_rx, b_tx, b_rx, a_tx, a_rx, swap_tx, swap_rx, out_b, out_a,
    send_sem, recv_sem, local_sem,
):
    s = lax.axis_index("seq")
    t = lax.axis_index("tp")
    y, xl, c = s // 4, lax.rem(s // 2, 2), lax.rem(s, 2)
    xh, z = t // 8, lax.rem(t, 8)

    def dev(dy=0, dx=0, dc=0, dh=0, dz=0):
        seq = lax.rem(y + dy, 4) * 4 + lax.rem(xl + dx, 2) * 2 + lax.rem(c + dc, 2)
        return (seq, lax.rem(xh + dh, 2) * 8 + lax.rem(z + dz + 8, 8))

    started = []
    counts = [0, 0]

    def send(src, dst, to):
        i = counts[0]
        counts[0] += 1
        copy = pltpu.make_async_remote_copy(
            src_ref=src, dst_ref=dst, send_sem=send_sem.at[i], recv_sem=recv_sem.at[i],
            device_id=to, device_id_type=MESH,
        )
        copy.start()
        started.append(copy)
        return copy

    def local(src, dst):
        i = counts[1]
        counts[1] += 1
        copy = pltpu.make_async_copy(src, dst, local_sem.at[i])
        copy.start()
        return copy

    load_tok = local(tok, tok_v)
    load_k = local(wk, wk_v)
    load_v = local(wv, wv_v)
    load_q = local(wq, wq_v)

    barrier = pltpu.get_barrier_semaphore()
    partners = [dev(dy=dy, dc=dc) for dy in range(4) for dc in range(2) if dy or dc]
    partners += [dev(dx=1, dc=dc) for dc in range(2)]
    partners += [dev(dz=1), dev(dz=-1), dev(dh=1)]
    for partner in partners:
        pl.semaphore_signal(barrier, inc=1, device_id=partner, device_id_type=MESH)
    def other(e):
        return lax.rem(c + e, 2)

    def query_rows(dy):
        return pl.ds(pl.multiple_of(((4 - dy) % 4) * 256 + c * 128, 128), 128)

    def key_rows(dx):
        return pl.ds(pl.multiple_of(dx * 256 + c * 128, 128), 128)

    near = [(1, 0), (1, 1), (3, 0), (3, 1)]
    order = [(0, 1), (2, 0), (2, 1)] + near

    def head_lanes(e):
        return pl.ds(pl.multiple_of(other(e) * 128, 128), 128)

    def project(weight, own):
        product = nn(tok_v[...], weight[...]).astype(BF16)
        for h in range(2):
            for a in range(SUB):
                own[h, a] = product[a * 128 : (a + 1) * 128, h * 128 : (h + 1) * 128]

    def share_keys(own, everyone):
        copies = {(0, 0): local(own.at[c], everyone.at[:, key_rows(0), :])}
        for dx, e in ((0, 1), (1, 0), (1, 1)):
            copies[dx, e] = send(own.at[other(e)], everyone.at[:, key_rows(dx), :], dev(dx=dx, dc=e))
        return copies

    load_tok.wait()
    load_k.wait()
    project(wk_v, k_own)
    load_v.wait()
    project(wv_v, v_own)
    load_q.wait()
    project(wq_v, q_own)
    pl.semaphore_wait(barrier, len(partners))
    got_q = {(0, 0): local(q_own.at[c], q_all.at[:, query_rows(0), :])}
    got_do = {(0, 0): local(do.at[:, :, head_lanes(0)], do_all.at[:, query_rows(0), :])}

    def share_q(dy, e):
        got_q[dy, e] = send(q_own.at[other(e)], q_all.at[:, query_rows(dy), :], dev(dy=dy, dc=e))

    def share_do(dy, e):
        got_do[dy, e] = send(
            do.at[:, :, head_lanes(e)], do_all.at[:, query_rows(dy), :], dev(dy=dy, dc=e)
        )

    got_k = share_keys(k_own, k_all)
    share_q(0, 1)
    for e in range(2):
        share_q(1, e)
        share_do(3, e)
    got_v = share_keys(v_own, v_all)
    share_do(0, 1)
    for e in range(2):
        share_do(1, e)
        share_q(3, e)

    row = lax.broadcasted_iota(jnp.int32, (512, 256), 0)
    key_time[...] = (row & 127) * 16 + y * 4 + lax.rem(xl + (row >> 8), 2) * 2 + ((row >> 7) & 1)
    tops[...] = jnp.full(tops.shape, FLOOR, F32)
    totals[...] = jnp.zeros(totals.shape, F32)
    moments[...] = jnp.zeros(moments.shape, F32)

    def arrived(copies, place):
        for e in range(2):
            if place == 0 and e == 0:
                copies[0, 0].wait()
            else:
                copies[place, e].wait_recv()

    exponent = SCALE * LOG2E

    def tiles(dq, f):
        lanes = slice(dq * 256, (dq + 1) * 256)
        rows = slice(f * 256, (f + 1) * 256)
        col = lax.broadcasted_iota(jnp.int32, (1, 256), 1)
        query_time = (col & 127) * 16 + lax.rem(y + dq, 4) * 4 + xl * 2 + (col >> 7)

        def tile(a, j, slot, masked):
            scores = nt(k_all[j, rows, :], q_all[a, lanes, :])
            if masked:
                scores = jnp.where(key_time[rows, :] <= query_time, scores, NEG)
            top = jnp.maximum(jnp.max(scores, axis=0, keepdims=True), FLOOR)
            weights = jnp.exp2((scores - top) * exponent)
            grad_probs = nt(v_all[j, rows, :], do_all[a, lanes, :])
            place = pl.ds(j * 2 + f, 1)
            tops[a, place, lanes] = top
            totals[a, place, lanes] = jnp.sum(weights, axis=0, keepdims=True)
            moments[a, place, lanes] = jnp.sum(weights * grad_probs, axis=0, keepdims=True)
            w_s[slot, rows, lanes] = weights.astype(BF16)
            dp_s[slot, rows, lanes] = grad_probs.astype(BF16)

        @pl.loop(0, 3)
        def _(i):
            tile(i, i, i, True)
            tile((i + 3) // 2, i // 2, i + 3, False)

    arrived(got_k, 0)
    arrived(got_v, 0)
    arrived(got_q, 0)
    arrived(got_do, 0)
    tiles(0, 0)
    arrived(got_q, 1)
    relay_q = send(q_all.at[:, 768:1024, :], q_all.at[:, 512:768, :], dev(dy=1))
    arrived(got_do, 3)
    relay_do = send(do_all.at[:, 256:512, :], do_all.at[:, 512:768, :], dev(dy=3))
    arrived(got_do, 1)
    tiles(3, 0)
    arrived(got_q, 3)
    tiles(1, 0)
    arrived(got_k, 1)
    arrived(got_v, 1)
    for dq in (0, 3, 1):
        tiles(dq, 1)
    for a in range(SUB):
        k_t[a] = k_all[a].T
    relay_q.wait_recv()
    relay_do.wait_recv()
    tiles(2, 0)
    tiles(2, 1)

    def slots_of(a):
        return [(j, a if j == a else 2 + a + j) for j in range(a + 1)]

    row_tx[...] = jnp.zeros(row_tx.shape, F32)
    for a in range(SUB):
        top = jnp.max(tops[a], axis=0, keepdims=True)
        factor = jnp.exp2((tops[a] - top) * exponent)
        total = jnp.maximum(jnp.sum(totals[a] * factor, axis=0, keepdims=True), 1e-30)
        moment = jnp.sum(moments[a] * factor, axis=0, keepdims=True)
        row_tx[a : a + 1, :] = top * exponent + jnp.log(total) * LOG2E
        row_tx[4 + a : 5 + a, :] = moment / total
    got_rows = {dy: send(row_tx, row_rx.at[3 - dy], dev(dy=dy)) for dy in (2, 1, 3)}
    for dy in (1, 3, 2):
        got_rows[dy].wait_recv()
    for dq in range(4):
        lanes = slice(dq * 256, (dq + 1) * 256)
        sums = [row_tx[0:4, lanes]]
        deltas = [row_tx[4:8, lanes]]
        for dy in (1, 2, 3):
            there = ((dq - dy) % 4) * 256
            sums.append(row_rx[dy - 1, 0:4, there : there + 256])
            deltas.append(row_rx[dy - 1, 4:8, there : there + 256])
        top = functools.reduce(jnp.maximum, sums)
        parts = [jnp.exp2(v - top) for v in sums]
        total = sum(parts)
        row_all[0:4, lanes] = top + LOG2E * jnp.log(total)
        row_all[4:8, lanes] = sum(v * part for v, part in zip(deltas, parts)) / total

    got_dq = []
    got_dkv = []
    kept = []
    turn = 0
    for a in (2, 1, 0):
        delta = row_all[4 + a : 5 + a, :]
        factor = jnp.exp2(tops[a] * exponent - row_all[a : a + 1, :])
        grad_q = None
        for j, slot in reversed(slots_of(a)):
            side = turn % 2
            turn += 1
            for dq, f in [(dq, f) for dq in range(4) for f in range(2)]:
                lanes = slice(dq * 256, (dq + 1) * 256)
                rows = slice(f * 256, (f + 1) * 256)
                place = slice(j * 2 + f, j * 2 + f + 1)
                probs = w_s[slot, rows, lanes].astype(F32) * factor[place, lanes]
                p_buf[side, rows, lanes] = probs.astype(BF16)
                ds_buf[side, rows, lanes] = (
                    probs * (dp_s[slot, rows, lanes].astype(F32) - delta[:, lanes])
                ).astype(BF16)
            part_v = nn(p_buf[side], do_all[a])
            part_k = nn(ds_buf[side], q_all[a])
            part_q = nn(k_t[j], ds_buf[side])
            grad_q = part_q if grad_q is None else grad_q + part_q
            if a == 2:
                dv_acc[j] = part_v
                dk_acc[j] = part_k
            else:
                dv_acc[j] += part_v
                dk_acc[j] += part_k
        dkv_tx[a, :, 0] = (dk_acc[a] * SCALE).astype(BF16).reshape(4, 128, 128)
        dkv_tx[a, :, 1] = dv_acc[a].astype(BF16).reshape(4, 128, 128)
        dq_tx[a] = (grad_q * SCALE).T.astype(BF16).reshape(4, 2, 128, 128)
        for dx, e in ((1, 0), (1, 1), (0, 1), (0, 0)):
            src = dkv_tx.at[a, dx * 2 + other(e)]
            dst = dkv_rx.at[a, dx, e]
            if dx or e:
                got_dkv.append(send(src, dst, dev(dx=dx, dc=e)))
            else:
                kept.append(local(src, dst))
        for dy, e in order + [(0, 0)]:
            src = dq_tx.at[a, dy, other(e)]
            dst = dq_rx.at[a, (4 - dy) % 4, e]
            if dy or e:
                got_dq.append(send(src, dst, dev(dy=dy, dc=e)))
            else:
                kept.append(local(src, dst))
    for copy in got_dq + got_dkv:
        copy.wait_recv()
    for copy in kept:
        copy.wait()
    for a in range(SUB):
        rows = slice(a * 128, (a + 1) * 128)
        for e in range(2):
            base = pl.multiple_of(other(e) * 128, 128)
            total = sum(dq_rx[a, i, e].astype(F32) for i in range(4))
            grads[0, rows, pl.ds(base, 128)] = total.astype(BF16)
            for i in range(2):
                total = dkv_rx[a, 0, e, i].astype(F32) + dkv_rx[a, 1, e, i].astype(F32)
                grads[1 + i, rows, pl.ds(base, 128)] = total.astype(BF16)

    def far(r):
        return lax.rem(z + r + 8, 8)

    def product(rows, start, width):
        places = pl.ds(pl.multiple_of(start, 128), width)
        weights = (wq_v, wk_v, wv_v)
        return sum(nt(grads[i, rows, :], weights[i][places, :]) for i in range(3))

    far_way = {0: 0, 1: 1}
    pieces = [slice(p * HALF, (p + 1) * HALF) for p in far_way]

    def rows_of(p, ref, *index):
        return ref.at[(*index, pieces[p], slice(None))]

    def part_b(r, rows):
        return product(rows, 2048 + far(r) * 256, 256)

    def part_a(r, dh, rows):
        return product(rows, lax.rem(xh + dh, 2) * 1024 + far(r) * 128, 128)

    got_x = {}
    arrived_x = set()

    def send_x(r):
        x_tx[r + 3] = part_a(r, 1, slice(None)).astype(BF16)
        got_x[r] = send(x_tx.at[r + 3], x_rx.at[r + 3], dev(dh=1))

    def own_a(r, rows):
        term = part_a(r, 0, rows)
        if r not in arrived_x:
            arrived_x.add(r)
            got_x[r].wait_recv()
        return term + x_rx[r + 3, rows, :].astype(F32)

    class Ring:
        def __init__(self, own, tx, rx):
            self.own, self.tx, self.rx, self.got = own, tx, rx, {}

        def hop(self, w, step, p):
            value = self.own((4 - step) * (1 - 2 * w) if step else 4, pieces[p])
            if (w, step - 1, p) in self.got:
                self.got[w, step - 1, p].wait_recv()
                value += self.rx[w, step - 1, pieces[p], :].astype(F32)
            self.tx[w, step, pieces[p], :] = value.astype(BF16)
            self.got[w, step, p] = send(
                rows_of(p, self.tx, w, step), rows_of(p, self.rx, w, step), dev(dz=1 - 2 * w)
            )

        def wave(self, k):
            for early in (True, False):
                for p, way in far_way.items():
                    for w in range(2):
                        step = k if way == w else k + 1
                        if (way == w) == early and step < 4:
                            self.hop(w, step, p)

        def last(self, p):
            value = self.own(0, pieces[p])
            for w in range(2):
                self.got[w, 3, p].wait_recv()
                value += self.rx[w, 3, pieces[p], :].astype(F32)
            return value

    ring_b = Ring(part_b, b_tx, b_rx)
    ring_a = Ring(own_a, a_tx, a_rx)
    send_x(4)
    ring_b.wave(0)
    for r in (3, -3, 2, -2, 1, -1, 0):
        send_x(r)
    ring_b.wave(1)
    ring_a.wave(0)
    ring_b.wave(2)
    ring_a.wave(1)
    ring_b.wave(3)
    ring_a.wave(2)
    got_swap = []
    for p in far_way:
        swap_tx[pieces[p], :] = ring_b.last(p).astype(BF16)
        got_swap.append(send(rows_of(p, swap_tx), rows_of(p, swap_rx), dev(dh=1)))
    ring_a.wave(3)

    stores = []
    gather_b, gather_a = {}, {}
    got_across = {}

    def store_b(r):
        i = far(r)
        lanes = pl.ds(pl.multiple_of(2048 + i * 256, 128), 256)
        stores.append(local(out_b.at[i], out.at[:, lanes]))

    def store_a(r, dh):
        i, h = far(r), lax.rem(xh + dh, 2)
        lanes = pl.ds(pl.multiple_of(h * 1024 + i * 128, 128), 128)
        stores.append(local(out_a.at[h, i], out.at[:, lanes]))

    def pass_on(got, buf, w, step, p):
        if step:
            got[w, step - 1, p].wait_recv()
        if step < 3 or (step == 3 and far_way[p] == w):
            piece = rows_of(p, buf, far(-step * (1 - 2 * w)))
            got[w, step, p] = send(piece, piece, dev(dz=1 - 2 * w))

    def across(r):
        i = far(r)
        got_across[r] = send(out_a.at[xh, i], out_a.at[xh, i], dev(dh=1))

    own_out_a = out_a.at[xh]
    for p in far_way:
        out_a[xh, z, pieces[p], :] = ring_a.last(p).astype(BF16)
        for w in range(2):
            pass_on(gather_a, own_out_a, w, 0, p)
    across(0)
    store_a(0, 0)
    for p in far_way:
        got_swap[p].wait_recv()
        out_b[z, pieces[p], :] = (
            swap_tx[pieces[p], :].astype(F32) + swap_rx[pieces[p], :].astype(F32)
        ).astype(BF16)
        for w in range(2):
            pass_on(gather_b, out_b, w, 0, p)
    store_b(0)
    for step in range(1, 4):
        for got, buf in ((gather_a, own_out_a), (gather_b, out_b)):
            for p in far_way:
                for w in range(2):
                    pass_on(got, buf, w, step, p)
            for r in (-step, step):
                if got is gather_a:
                    across(r)
                    store_a(r, 0)
                else:
                    store_b(r)
    for p, w in far_way.items():
        gather_a[w, 3, p].wait_recv()
    across(4)
    store_a(4, 0)
    for p, w in far_way.items():
        gather_b[w, 3, p].wait_recv()
    store_b(4)
    for r in (0, -1, 1, -2, 2, -3, 3, 4):
        got_across[r].wait_recv()
        store_a(r, 1)
    for copy in stores:
        copy.wait()
    for copy in started:
        copy.wait_send()


def shards(tokens, w_query, w_key, w_value, grad_out):
    anywhere = pl.BlockSpec(memory_space=pl.ANY)
    scratch = [
        ((ROWS, D), BF16), ((D, 256), BF16), ((D, 256), BF16), ((D, 256), BF16),
        ((2, SUB, 128, 128), BF16), ((2, SUB, 128, 128), BF16), ((2, SUB, 128, 128), BF16),
        ((SUB, 1024, 128), BF16), ((SUB, 1024, 128), BF16),
        ((SUB, 512, 128), BF16), ((SUB, 512, 128), BF16), ((SUB, 128, 512), BF16),
        ((512, 256), jnp.int32), ((6, 512, 1024), BF16), ((6, 512, 1024), BF16),
        ((SUB, 8, 1024), F32), ((SUB, 8, 1024), F32), ((SUB, 8, 1024), F32), ((8, 1024), F32), ((3, 8, 1024), F32), ((8, 1024), F32),
        ((2, 512, 1024), BF16), ((2, 512, 1024), BF16), ((SUB, 512, 128), F32), ((SUB, 512, 128), F32),
        ((SUB, 4, 2, 128, 128), BF16), ((SUB, 4, 2, 128, 128), BF16),
        ((SUB, 4, 2, 128, 128), BF16), ((SUB, 2, 2, 2, 128, 128), BF16), ((3, ROWS, 256), BF16),
        ((8, ROWS, 128), BF16), ((8, ROWS, 128), BF16),
        ((2, 4, ROWS, 256), BF16), ((2, 4, ROWS, 256), BF16),
        ((2, 4, ROWS, 128), BF16), ((2, 4, ROWS, 128), BF16),
        ((ROWS, 256), BF16), ((ROWS, 256), BF16),
        ((8, ROWS, 256), BF16), ((2, 8, ROWS, 128), BF16),
    ]
    return pl.pallas_call(
        kernel,
        out_shape=jax.ShapeDtypeStruct((ROWS, D), BF16),
        in_specs=[anywhere] * 5,
        out_specs=anywhere,
        scratch_shapes=[pltpu.VMEM(shape, kind) for shape, kind in scratch]
        + [
            pltpu.SemaphoreType.DMA((COPIES,)),
            pltpu.SemaphoreType.DMA((COPIES,)),
            pltpu.SemaphoreType.DMA((LOCALS,)),
        ],
        compiler_params=pltpu.CompilerParams(
            collective_id=0, has_side_effects=True, vmem_limit_bytes=60 * 2**20
        ),
    )(tokens, w_query, w_key, w_value, grad_out.reshape(SUB, 128, 256))


def solution(mesh):
    placed = (P("seq", None), P(None, "tp"), P(None, "tp"), P(None, "tp"), P("seq", "tp"))
    return jax.shard_map(
        shards, mesh=mesh, in_specs=placed, out_specs=P("seq", None), check_vma=False
    )
```

```python
import functools

import jax
import jax.numpy as jnp
from jax import lax
from jax.experimental import pallas as pl
from jax.experimental.pallas import tpu as pltpu
from jax.sharding import PartitionSpec as P

MESH = pl.DeviceIdType.MESH
HEAD = 128
ROWS = 384
D = 4096
SUB = 3
F32 = jnp.float32
BF16 = jnp.bfloat16
LOG2E = 1.4426950408889634
SCALE = HEAD ** (-0.5)
NEG = -1e30
FLOOR = -1e29
COPIES = 240
LOCALS = 48


def nt(a, b):
    return lax.dot_general(a, b, (((1,), (1,)), ((), ())), preferred_element_type=F32)


def nn(a, b):
    return jnp.dot(a, b, preferred_element_type=F32)


def kernel(
    tok, wq, wk, wv, do, out,
    tok_v, wq_v, wk_v, wv_v,
    q_own, k_own, v_own,
    q_all, do_all, k_all, v_all, k_t,
    key_time, w_s, dp_s, tops, totals, moments, row_tx, row_rx, row_all,
    p_buf, ds_buf, dk_acc, dv_acc,
    dq_tx, dkv_tx, dq_rx, dkv_rx, grads,
    x_tx, x_rx, a_own, b_tx, b_rx, a_tx, a_rx, swap_tx, swap_rx, out_b, out_a,
    send_sem, recv_sem, local_sem,
):
    s = lax.axis_index("seq")
    t = lax.axis_index("tp")
    y, xl, c = s // 4, lax.rem(s // 2, 2), lax.rem(s, 2)
    xh, z = t // 8, lax.rem(t, 8)

    def dev(dy=0, dx=0, dc=0, dh=0, dz=0):
        seq = lax.rem(y + dy, 4) * 4 + lax.rem(xl + dx, 2) * 2 + lax.rem(c + dc, 2)
        return (seq, lax.rem(xh + dh, 2) * 8 + lax.rem(z + dz + 8, 8))

    started = []
    counts = [0, 0]

    def send(src, dst, to):
        i = counts[0]
        counts[0] += 1
        copy = pltpu.make_async_remote_copy(
            src_ref=src, dst_ref=dst, send_sem=send_sem.at[i], recv_sem=recv_sem.at[i],
            device_id=to, device_id_type=MESH,
        )
        copy.start()
        started.append(copy)
        return copy

    def local(src, dst):
        i = counts[1]
        counts[1] += 1
        copy = pltpu.make_async_copy(src, dst, local_sem.at[i])
        copy.start()
        return copy

    load_tok = local(tok, tok_v)
    load_k = local(wk, wk_v)
    load_v = local(wv, wv_v)
    load_q = local(wq, wq_v)

    barrier = pltpu.get_barrier_semaphore()
    partners = [dev(dy=dy, dc=dc) for dy in range(4) for dc in range(2) if dy or dc]
    partners += [dev(dx=1, dc=dc) for dc in range(2)]
    partners += [dev(dz=1), dev(dz=-1), dev(dh=1)]
    for partner in partners:
        pl.semaphore_signal(barrier, inc=1, device_id=partner, device_id_type=MESH)
    def other(e):
        return lax.rem(c + e, 2)

    def query_rows(dy):
        return pl.ds(pl.multiple_of(((4 - dy) % 4) * 256 + c * 128, 128), 128)

    def key_rows(dx):
        return pl.ds(pl.multiple_of(dx * 256 + c * 128, 128), 128)

    near = [(1, 0), (1, 1), (3, 0), (3, 1)]
    order = [(0, 1), (2, 0), (2, 1)] + near

    def head_lanes(e):
        return pl.ds(pl.multiple_of(other(e) * 128, 128), 128)

    def project(weight, own):
        product = nn(tok_v[...], weight[...]).astype(BF16)
        for h in range(2):
            for a in range(SUB):
                own[h, a] = product[a * 128 : (a + 1) * 128, h * 128 : (h + 1) * 128]

    def share_keys(own, everyone):
        copies = {(0, 0): local(own.at[c], everyone.at[:, key_rows(0), :])}
        for dx, e in ((0, 1), (1, 0), (1, 1)):
            copies[dx, e] = send(own.at[other(e)], everyone.at[:, key_rows(dx), :], dev(dx=dx, dc=e))
        return copies

    load_tok.wait()
    load_k.wait()
    project(wk_v, k_own)
    load_v.wait()
    project(wv_v, v_own)
    load_q.wait()
    project(wq_v, q_own)
    pl.semaphore_wait(barrier, len(partners))
    got_q = {(0, 0): local(q_own.at[c], q_all.at[:, query_rows(0), :])}
    got_do = {(0, 0): local(do.at[:, :, head_lanes(0)], do_all.at[:, query_rows(0), :])}

    def share_q(dy, e):
        got_q[dy, e] = send(q_own.at[other(e)], q_all.at[:, query_rows(dy), :], dev(dy=dy, dc=e))

    def share_do(dy, e):
        got_do[dy, e] = send(
            do.at[:, :, head_lanes(e)], do_all.at[:, query_rows(dy), :], dev(dy=dy, dc=e)
        )

    got_k = share_keys(k_own, k_all)
    share_q(0, 1)
    for e in range(2):
        share_q(1, e)
        share_do(3, e)
    got_v = share_keys(v_own, v_all)
    share_do(0, 1)
    for e in range(2):
        share_do(1, e)
        share_q(3, e)

    row = lax.broadcasted_iota(jnp.int32, (512, 256), 0)
    key_time[...] = (row & 127) * 16 + y * 4 + lax.rem(xl + (row >> 8), 2) * 2 + ((row >> 7) & 1)
    tops[...] = jnp.full(tops.shape, FLOOR, F32)
    totals[...] = jnp.zeros(totals.shape, F32)
    moments[...] = jnp.zeros(moments.shape, F32)

    def arrived(copies, place):
        for e in range(2):
            if place == 0 and e == 0:
                copies[0, 0].wait()
            else:
                copies[place, e].wait_recv()

    exponent = SCALE * LOG2E

    def tiles(dq, f):
        lanes = slice(dq * 256, (dq + 1) * 256)
        rows = slice(f * 256, (f + 1) * 256)
        col = lax.broadcasted_iota(jnp.int32, (1, 256), 1)
        query_time = (col & 127) * 16 + lax.rem(y + dq, 4) * 4 + xl * 2 + (col >> 7)

        def tile(a, j, slot, masked):
            scores = nt(k_all[j, rows, :], q_all[a, lanes, :])
            if masked:
                scores = jnp.where(key_time[rows, :] <= query_time, scores, NEG)
            top = jnp.maximum(jnp.max(scores, axis=0, keepdims=True), FLOOR)
            weights = jnp.exp2((scores - top) * exponent)
            grad_probs = nt(v_all[j, rows, :], do_all[a, lanes, :])
            place = pl.ds(j * 2 + f, 1)
            tops[a, place, lanes] = top
            totals[a, place, lanes] = jnp.sum(weights, axis=0, keepdims=True)
            moments[a, place, lanes] = jnp.sum(weights * grad_probs, axis=0, keepdims=True)
            w_s[slot, rows, lanes] = weights.astype(BF16)
            dp_s[slot, rows, lanes] = grad_probs.astype(BF16)

        @pl.loop(0, 3)
        def _(i):
            tile(i, i, i, True)
            tile((i + 3) // 2, i // 2, i + 3, False)

    arrived(got_k, 0)
    arrived(got_v, 0)
    arrived(got_q, 0)
    arrived(got_do, 0)
    tiles(0, 0)
    arrived(got_q, 1)
    relay_q = send(q_all.at[:, 768:1024, :], q_all.at[:, 512:768, :], dev(dy=1))
    arrived(got_do, 3)
    relay_do = send(do_all.at[:, 256:512, :], do_all.at[:, 512:768, :], dev(dy=3))
    arrived(got_do, 1)
    tiles(3, 0)
    arrived(got_q, 3)
    tiles(1, 0)
    arrived(got_k, 1)
    arrived(got_v, 1)
    for dq in (0, 3, 1):
        tiles(dq, 1)
    for a in range(SUB):
        k_t[a] = k_all[a].T
    relay_q.wait_recv()
    relay_do.wait_recv()
    tiles(2, 0)
    tiles(2, 1)

    def slots_of(a):
        return [(j, a if j == a else 2 + a + j) for j in range(a + 1)]

    row_tx[...] = jnp.zeros(row_tx.shape, F32)
    for a in range(SUB):
        top = jnp.max(tops[a], axis=0, keepdims=True)
        factor = jnp.exp2((tops[a] - top) * exponent)
        total = jnp.maximum(jnp.sum(totals[a] * factor, axis=0, keepdims=True), 1e-30)
        moment = jnp.sum(moments[a] * factor, axis=0, keepdims=True)
        row_tx[a : a + 1, :] = top * exponent + jnp.log(total) * LOG2E
        row_tx[4 + a : 5 + a, :] = moment / total
    got_rows = {dy: send(row_tx, row_rx.at[3 - dy], dev(dy=dy)) for dy in (2, 1, 3)}
    for dy in (1, 3, 2):
        got_rows[dy].wait_recv()
    for dq in range(4):
        lanes = slice(dq * 256, (dq + 1) * 256)
        sums = [row_tx[0:4, lanes]]
        deltas = [row_tx[4:8, lanes]]
        for dy in (1, 2, 3):
            there = ((dq - dy) % 4) * 256
            sums.append(row_rx[dy - 1, 0:4, there : there + 256])
            deltas.append(row_rx[dy - 1, 4:8, there : there + 256])
        top = functools.reduce(jnp.maximum, sums)
        parts = [jnp.exp2(v - top) for v in sums]
        total = sum(parts)
        row_all[0:4, lanes] = top + LOG2E * jnp.log(total)
        row_all[4:8, lanes] = sum(v * part for v, part in zip(deltas, parts)) / total

    got_grads = {a: [] for a in range(SUB)}
    kept = {a: [] for a in range(SUB)}
    turn = 0
    for a in (2, 1, 0):
        delta = row_all[4 + a : 5 + a, :]
        factor = jnp.exp2(tops[a] * exponent - row_all[a : a + 1, :])
        grad_q = None
        for j, slot in reversed(slots_of(a)):
            side = turn % 2
            turn += 1
            for dq, f in [(dq, f) for dq in range(4) for f in range(2)]:
                lanes = slice(dq * 256, (dq + 1) * 256)
                rows = slice(f * 256, (f + 1) * 256)
                place = slice(j * 2 + f, j * 2 + f + 1)
                probs = w_s[slot, rows, lanes].astype(F32) * factor[place, lanes]
                p_buf[side, rows, lanes] = probs.astype(BF16)
                ds_buf[side, rows, lanes] = (
                    probs * (dp_s[slot, rows, lanes].astype(F32) - delta[:, lanes])
                ).astype(BF16)
            part_v = nn(p_buf[side], do_all[a])
            part_k = nn(ds_buf[side], q_all[a])
            part_q = nn(k_t[j], ds_buf[side])
            grad_q = part_q if grad_q is None else grad_q + part_q
            if a == 2:
                dv_acc[j] = part_v
                dk_acc[j] = part_k
            else:
                dv_acc[j] += part_v
                dk_acc[j] += part_k
        dkv_tx[a, :, 0] = (dk_acc[a] * SCALE).astype(BF16).reshape(4, 128, 128)
        dkv_tx[a, :, 1] = dv_acc[a].astype(BF16).reshape(4, 128, 128)
        dq_tx[a] = (grad_q * SCALE).T.astype(BF16).reshape(4, 2, 128, 128)
        for dx, e in ((1, 0), (1, 1), (0, 1), (0, 0)):
            src = dkv_tx.at[a, dx * 2 + other(e)]
            dst = dkv_rx.at[a, dx, e]
            if dx or e:
                got_grads[a].append(send(src, dst, dev(dx=dx, dc=e)))
            else:
                kept[a].append(local(src, dst))
        for dy, e in order + [(0, 0)]:
            src = dq_tx.at[a, dy, other(e)]
            dst = dq_rx.at[a, (4 - dy) % 4, e]
            if dy or e:
                got_grads[a].append(send(src, dst, dev(dy=dy, dc=e)))
            else:
                kept[a].append(local(src, dst))
    def finish_grads(a):
        for copy in got_grads[a]:
            copy.wait_recv()
        for copy in kept[a]:
            copy.wait()
        rows = slice(a * 128, (a + 1) * 128)
        for e in range(2):
            base = pl.multiple_of(other(e) * 128, 128)
            total = sum(dq_rx[a, i, e].astype(F32) for i in range(4))
            grads[0, rows, pl.ds(base, 128)] = total.astype(BF16)
            for i in range(2):
                total = dkv_rx[a, 0, e, i].astype(F32) + dkv_rx[a, 1, e, i].astype(F32)
                grads[1 + i, rows, pl.ds(base, 128)] = total.astype(BF16)

    blocks = (2, 1, 0)
    pieces = [slice(a * 128, (a + 1) * 128) for a in blocks]

    def far(r):
        return lax.rem(z + r + 8, 8)

    def product(p, start, width):
        places = pl.ds(pl.multiple_of(start, 128), width)
        weights = (wq_v, wk_v, wv_v)
        return sum(nt(grads[i, pieces[p], :], weights[i][places, :]) for i in range(3))

    def rows_of(p, ref, *index):
        return ref.at[(*index, pieces[p], slice(None))]

    got_x = {}

    def start_x(p):
        theirs = product(p, lax.rem(xh + 1, 2) * 1024, 1024).astype(BF16)
        for i in range(8):
            x_tx[i, pieces[p], :] = theirs[:, i * 128 : (i + 1) * 128]
        mine = product(p, xh * 1024, 1024)
        for i in range(8):
            a_own[i, pieces[p], :] = mine[:, i * 128 : (i + 1) * 128]

    def more_x(p, places):
        for r in places:
            i = far(r)
            got_x[r, p] = send(rows_of(p, x_tx, i), rows_of(p, x_rx, i), dev(dh=1))

    def own_b(r, p):
        return product(p, 2048 + far(r) * 256, 256)

    used_x = set()

    def own_a(r, p):
        if (r, p) not in used_x:
            used_x.add((r, p))
            got_x[r, p].wait_recv()
        i = far(r)
        return a_own[i, pieces[p], :] + x_rx[i, pieces[p], :].astype(F32)

    class Ring:
        def __init__(self, own, tx, rx, far_way):
            self.own, self.tx, self.rx, self.far_way, self.got = own, tx, rx, far_way, {}

        def hop(self, w, step, p):
            value = self.own((4 - step) * (1 - 2 * w) if step else 4, p)
            if (w, step - 1, p) in self.got:
                self.got[w, step - 1, p].wait_recv()
                value += self.rx[w, step - 1, pieces[p], :].astype(F32)
            self.tx[w, step, pieces[p], :] = value.astype(BF16)
            self.got[w, step, p] = send(
                rows_of(p, self.tx, w, step), rows_of(p, self.rx, w, step), dev(dz=1 - 2 * w)
            )

        def wave(self, k, p):
            way = self.far_way[p]
            self.hop(way, k, p)
            if k < 3:
                self.hop(1 - way, k + 1, p)

        def last(self, p):
            value = self.own(0, p)
            for w in range(2):
                self.got[w, 3, p].wait_recv()
                value += self.rx[w, 3, pieces[p], :].astype(F32)
            return value

    ring_b = Ring(own_b, b_tx, b_rx, (0, 1, 0))
    ring_a = Ring(own_a, a_tx, a_rx, (0, 1, 1))
    stores = []
    got_swap = {}
    gather_b, gather_a = {}, {}
    got_across = {}
    own_out_a = out_a.at[xh]

    def store_b(r):
        i = far(r)
        lanes = pl.ds(pl.multiple_of(2048 + i * 256, 128), 256)
        stores.append(local(out_b.at[i], out.at[:, lanes]))

    def store_a(r, dh):
        i, h = far(r), lax.rem(xh + dh, 2)
        lanes = pl.ds(pl.multiple_of(h * 1024 + i * 128, 128), 128)
        stores.append(local(out_a.at[h, i], out.at[:, lanes]))

    def pass_on(got, buf, far_way, step, p):
        for w in range(2):
            if step and (step < 4 or far_way[p] == w):
                got[w, step - 1, p].wait_recv()
            if step < 3 or (step == 3 and far_way[p] == w):
                piece = rows_of(p, buf, far(-step * (1 - 2 * w)))
                got[w, step, p] = send(piece, piece, dev(dz=1 - 2 * w))

    def places(step):
        return [0] if step == 0 else [4] if step == 4 else [-step, step]

    def stage_b(k, p):
        if k < 4:
            ring_b.wave(k, p)
        elif k == 4:
            swap_tx[pieces[p], :] = ring_b.last(p).astype(BF16)
            got_swap[p] = send(rows_of(p, swap_tx), rows_of(p, swap_rx), dev(dh=1))
        elif k < 10:
            if k == 5:
                got_swap[p].wait_recv()
                out_b[z, pieces[p], :] = (
                    swap_tx[pieces[p], :].astype(F32) + swap_rx[pieces[p], :].astype(F32)
                ).astype(BF16)
            pass_on(gather_b, out_b, ring_b.far_way, k - 5, p)
            if p == 2:
                for r in places(k - 5):
                    store_b(r)

    def stage_a(k, p):
        if k < 4:
            ring_a.wave(k, p)
        elif k < 9:
            if k == 4:
                out_a[xh, z, pieces[p], :] = ring_a.last(p).astype(BF16)
            pass_on(gather_a, own_out_a, ring_a.far_way, k - 4, p)
            for r in places(k - 4):
                piece = rows_of(p, out_a, xh, far(r))
                got_across[r, p] = send(piece, piece, dev(dh=1))
                if p == 2:
                    store_a(r, 0)

    offset = (0, 1, 1)
    for turn in range(12):
        for p in (0, 1, 2):
            if turn == offset[p]:
                finish_grads(blocks[p])
            if turn >= offset[p]:
                stage_b(turn - offset[p], p)
            if turn == offset[p]:
                start_x(p)
            if 0 <= turn - offset[p] < 4:
                more_x(p, ((4, 3, -3), (2, -2), (1, -1), (0,))[turn - offset[p]])
        for p in (0, 1, 2):
            if turn >= offset[p] + 1:
                stage_a(turn - offset[p] - 1, p)
    for r in (0, -1, 1, -2, 2, -3, 3, 4):
        for p in range(3):
            got_across[r, p].wait_recv()
        store_a(r, 1)
    for copy in stores:
        copy.wait()
    for copy in started:
        copy.wait_send()


def shards(tokens, w_query, w_key, w_value, grad_out):
    anywhere = pl.BlockSpec(memory_space=pl.ANY)
    scratch = [
        ((ROWS, D), BF16), ((D, 256), BF16), ((D, 256), BF16), ((D, 256), BF16),
        ((2, SUB, 128, 128), BF16), ((2, SUB, 128, 128), BF16), ((2, SUB, 128, 128), BF16),
        ((SUB, 1024, 128), BF16), ((SUB, 1024, 128), BF16),
        ((SUB, 512, 128), BF16), ((SUB, 512, 128), BF16), ((SUB, 128, 512), BF16),
        ((512, 256), jnp.int32), ((6, 512, 1024), BF16), ((6, 512, 1024), BF16),
        ((SUB, 8, 1024), F32), ((SUB, 8, 1024), F32), ((SUB, 8, 1024), F32), ((8, 1024), F32), ((3, 8, 1024), F32), ((8, 1024), F32),
        ((2, 512, 1024), BF16), ((2, 512, 1024), BF16), ((SUB, 512, 128), F32), ((SUB, 512, 128), F32),
        ((SUB, 4, 2, 128, 128), BF16), ((SUB, 4, 2, 128, 128), BF16),
        ((SUB, 4, 2, 128, 128), BF16), ((SUB, 2, 2, 2, 128, 128), BF16), ((3, ROWS, 256), BF16),
        ((8, ROWS, 128), BF16), ((8, ROWS, 128), BF16), ((8, ROWS, 128), F32),
        ((2, 4, ROWS, 256), BF16), ((2, 4, ROWS, 256), BF16),
        ((2, 4, ROWS, 128), BF16), ((2, 4, ROWS, 128), BF16),
        ((ROWS, 256), BF16), ((ROWS, 256), BF16),
        ((8, ROWS, 256), BF16), ((2, 8, ROWS, 128), BF16),
    ]
    return pl.pallas_call(
        kernel,
        out_shape=pltpu.VMEM((ROWS, D), BF16),
        in_specs=[anywhere] * 5,
        out_specs=pl.BlockSpec(memory_space=pltpu.VMEM),
        scratch_shapes=[pltpu.VMEM(shape, kind) for shape, kind in scratch]
        + [
            pltpu.SemaphoreType.DMA((COPIES,)),
            pltpu.SemaphoreType.DMA((COPIES,)),
            pltpu.SemaphoreType.DMA((LOCALS,)),
        ],
        compiler_params=pltpu.CompilerParams(
            collective_id=0, has_side_effects=True, vmem_limit_bytes=54 * 2**20
        ),
    )(tokens, w_query, w_key, w_value, grad_out.reshape(SUB, 128, 256))


def solution(mesh):
    placed = (P("seq", None), P(None, "tp"), P(None, "tp"), P(None, "tp"), P("seq", "tp"))
    return jax.shard_map(
        shards, mesh=mesh, in_specs=placed, out_specs=P("seq", None), check_vma=False
    )
```

```python
import functools

import jax
import jax.numpy as jnp
from jax import lax
from jax.experimental import pallas as pl
from jax.experimental.pallas import tpu as pltpu
from jax.sharding import PartitionSpec as P

MESH = pl.DeviceIdType.MESH
HEAD = 128
ROWS = 384
D = 4096
SUB = 3
F32 = jnp.float32
BF16 = jnp.bfloat16
LOG2E = 1.4426950408889634
SCALE = HEAD ** (-0.5)
NEG = -1e30
FLOOR = -1e29
COPIES = 240
LOCALS = 48


def nt(a, b):
    return lax.dot_general(a, b, (((1,), (1,)), ((), ())), preferred_element_type=F32)


def nn(a, b):
    return jnp.dot(a, b, preferred_element_type=F32)


def kernel(
    tok, wq, wk, wv, do, out,
    tok_v, wq_v, wk_v, wv_v,
    q_own, k_own, v_own,
    q_all, do_all, k_all, v_all, k_t,
    key_time, w_s, dp_s, tops, totals, moments, row_tx, row_rx, row_all,
    p_buf, ds_buf, dk_acc, dv_acc,
    dq_tx, dkv_tx, dq_rx, dkv_rx, grads,
    x_tx, x_rx, a_own, b_tx, b_rx, a_tx, a_rx, swap_tx, swap_rx, out_b, out_a,
    send_sem, recv_sem, local_sem,
):
    s = lax.axis_index("seq")
    t = lax.axis_index("tp")
    y, xl, c = s // 4, lax.rem(s // 2, 2), lax.rem(s, 2)
    xh, z = t // 8, lax.rem(t, 8)

    def dev(dy=0, dx=0, dc=0, dh=0, dz=0):
        seq = lax.rem(y + dy, 4) * 4 + lax.rem(xl + dx, 2) * 2 + lax.rem(c + dc, 2)
        return (seq, lax.rem(xh + dh, 2) * 8 + lax.rem(z + dz + 8, 8))

    started = []
    counts = [0, 0]

    def send(src, dst, to):
        i = counts[0]
        counts[0] += 1
        copy = pltpu.make_async_remote_copy(
            src_ref=src, dst_ref=dst, send_sem=send_sem.at[i], recv_sem=recv_sem.at[i],
            device_id=to, device_id_type=MESH,
        )
        copy.start()
        started.append(copy)
        return copy

    def local(src, dst):
        i = counts[1]
        counts[1] += 1
        copy = pltpu.make_async_copy(src, dst, local_sem.at[i])
        copy.start()
        return copy

    load_tok = local(tok, tok_v)
    load_k = local(wk, wk_v)
    load_v = local(wv, wv_v)
    load_q = local(wq, wq_v)

    barrier = pltpu.get_barrier_semaphore()
    partners = [dev(dy=dy, dc=dc) for dy in range(4) for dc in range(2) if dy or dc]
    partners += [dev(dx=1, dc=dc) for dc in range(2)]
    partners += [dev(dz=1), dev(dz=-1), dev(dh=1)]
    for partner in partners:
        pl.semaphore_signal(barrier, inc=1, device_id=partner, device_id_type=MESH)
    def other(e):
        return lax.rem(c + e, 2)

    def query_rows(dy):
        return pl.ds(pl.multiple_of(((4 - dy) % 4) * 256 + c * 128, 128), 128)

    def key_rows(dx):
        return pl.ds(pl.multiple_of(dx * 256 + c * 128, 128), 128)

    near = [(1, 0), (1, 1), (3, 0), (3, 1)]
    order = [(0, 1), (2, 0), (2, 1)] + near

    def head_lanes(e):
        return pl.ds(pl.multiple_of(other(e) * 128, 128), 128)

    def project(weight, own):
        product = nn(tok_v[...], weight[...]).astype(BF16)
        for h in range(2):
            for a in range(SUB):
                own[h, a] = product[a * 128 : (a + 1) * 128, h * 128 : (h + 1) * 128]

    def share_keys(own, everyone):
        copies = {(0, 0): local(own.at[c], everyone.at[:, key_rows(0), :])}
        for dx, e in ((0, 1), (1, 0), (1, 1)):
            copies[dx, e] = send(own.at[other(e)], everyone.at[:, key_rows(dx), :], dev(dx=dx, dc=e))
        return copies

    load_tok.wait()
    load_k.wait()
    project(wk_v, k_own)
    load_v.wait()
    project(wv_v, v_own)
    load_q.wait()
    project(wq_v, q_own)
    pl.semaphore_wait(barrier, len(partners))
    got_q = {(0, 0): local(q_own.at[c], q_all.at[:, query_rows(0), :])}
    got_do = {(0, 0): local(do.at[:, :, head_lanes(0)], do_all.at[:, query_rows(0), :])}

    def share_q(dy, e):
        got_q[dy, e] = send(q_own.at[other(e)], q_all.at[:, query_rows(dy), :], dev(dy=dy, dc=e))

    def share_do(dy, e):
        got_do[dy, e] = send(
            do.at[:, :, head_lanes(e)], do_all.at[:, query_rows(dy), :], dev(dy=dy, dc=e)
        )

    got_k = share_keys(k_own, k_all)
    share_q(0, 1)
    for e in range(2):
        share_q(1, e)
        share_do(3, e)
    got_v = share_keys(v_own, v_all)
    share_do(0, 1)
    for e in range(2):
        share_do(1, e)
        share_q(3, e)

    row = lax.broadcasted_iota(jnp.int32, (512, 256), 0)
    key_time[...] = (row & 127) * 16 + y * 4 + lax.rem(xl + (row >> 8), 2) * 2 + ((row >> 7) & 1)
    tops[...] = jnp.full(tops.shape, FLOOR, F32)
    totals[...] = jnp.zeros(totals.shape, F32)
    moments[...] = jnp.zeros(moments.shape, F32)

    def arrived(copies, place):
        for e in range(2):
            if place == 0 and e == 0:
                copies[0, 0].wait()
            else:
                copies[place, e].wait_recv()

    exponent = SCALE * LOG2E

    def tiles(dq, f):
        lanes = slice(dq * 256, (dq + 1) * 256)
        rows = slice(f * 256, (f + 1) * 256)
        col = lax.broadcasted_iota(jnp.int32, (1, 256), 1)
        query_time = (col & 127) * 16 + lax.rem(y + dq, 4) * 4 + xl * 2 + (col >> 7)

        def tile(a, j, slot, masked):
            scores = nt(k_all[j, rows, :], q_all[a, lanes, :])
            if masked:
                scores = jnp.where(key_time[rows, :] <= query_time, scores, NEG)
            top = jnp.maximum(jnp.max(scores, axis=0, keepdims=True), FLOOR)
            weights = jnp.exp2((scores - top) * exponent)
            grad_probs = nt(v_all[j, rows, :], do_all[a, lanes, :])
            place = pl.ds(j * 2 + f, 1)
            tops[a, place, lanes] = top
            totals[a, place, lanes] = jnp.sum(weights, axis=0, keepdims=True)
            moments[a, place, lanes] = jnp.sum(weights * grad_probs, axis=0, keepdims=True)
            w_s[slot, rows, lanes] = weights.astype(BF16)
            dp_s[slot, rows, lanes] = grad_probs.astype(BF16)

        @pl.loop(0, 3)
        def _(i):
            tile(i, i, i, True)
            tile((i + 3) // 2, i // 2, i + 3, False)

    arrived(got_k, 0)
    arrived(got_v, 0)
    arrived(got_q, 0)
    arrived(got_do, 0)
    tiles(0, 0)
    arrived(got_q, 1)
    relay_q = send(q_all.at[:, 768:1024, :], q_all.at[:, 512:768, :], dev(dy=1))
    arrived(got_do, 3)
    relay_do = send(do_all.at[:, 256:512, :], do_all.at[:, 512:768, :], dev(dy=3))
    arrived(got_do, 1)
    tiles(3, 0)
    arrived(got_q, 3)
    tiles(1, 0)
    arrived(got_k, 1)
    arrived(got_v, 1)
    for dq in (0, 3, 1):
        tiles(dq, 1)
    for a in range(SUB):
        k_t[a] = k_all[a].T
    relay_q.wait_recv()
    relay_do.wait_recv()
    tiles(2, 0)
    tiles(2, 1)

    def slots_of(a):
        return [(j, a if j == a else 2 + a + j) for j in range(a + 1)]

    row_tx[...] = jnp.zeros(row_tx.shape, F32)
    for a in range(SUB):
        top = jnp.max(tops[a], axis=0, keepdims=True)
        factor = jnp.exp2((tops[a] - top) * exponent)
        total = jnp.maximum(jnp.sum(totals[a] * factor, axis=0, keepdims=True), 1e-30)
        moment = jnp.sum(moments[a] * factor, axis=0, keepdims=True)
        row_tx[a : a + 1, :] = top * exponent + jnp.log(total) * LOG2E
        row_tx[4 + a : 5 + a, :] = moment / total
    got_rows = {dy: send(row_tx, row_rx.at[3 - dy], dev(dy=dy)) for dy in (2, 1, 3)}
    for dy in (1, 3, 2):
        got_rows[dy].wait_recv()
    for dq in range(4):
        lanes = slice(dq * 256, (dq + 1) * 256)
        sums = [row_tx[0:4, lanes]]
        deltas = [row_tx[4:8, lanes]]
        for dy in (1, 2, 3):
            there = ((dq - dy) % 4) * 256
            sums.append(row_rx[dy - 1, 0:4, there : there + 256])
            deltas.append(row_rx[dy - 1, 4:8, there : there + 256])
        top = functools.reduce(jnp.maximum, sums)
        parts = [jnp.exp2(v - top) for v in sums]
        total = sum(parts)
        row_all[0:4, lanes] = top + LOG2E * jnp.log(total)
        row_all[4:8, lanes] = sum(v * part for v, part in zip(deltas, parts)) / total

    got_grads = {a: [] for a in range(SUB)}
    kept = {a: [] for a in range(SUB)}
    turn = 0
    for a in (2, 1, 0):
        delta = row_all[4 + a : 5 + a, :]
        factor = jnp.exp2(tops[a] * exponent - row_all[a : a + 1, :])
        grad_q = None
        for j, slot in reversed(slots_of(a)):
            side = turn % 2
            turn += 1
            for dq, f in [(dq, f) for dq in range(4) for f in range(2)]:
                lanes = slice(dq * 256, (dq + 1) * 256)
                rows = slice(f * 256, (f + 1) * 256)
                place = slice(j * 2 + f, j * 2 + f + 1)
                probs = w_s[slot, rows, lanes].astype(F32) * factor[place, lanes]
                p_buf[side, rows, lanes] = probs.astype(BF16)
                ds_buf[side, rows, lanes] = (
                    probs * (dp_s[slot, rows, lanes].astype(F32) - delta[:, lanes])
                ).astype(BF16)
            part_v = nn(p_buf[side], do_all[a])
            part_k = nn(ds_buf[side], q_all[a])
            part_q = nn(k_t[j], ds_buf[side])
            grad_q = part_q if grad_q is None else grad_q + part_q
            if a == 2:
                dv_acc[j] = part_v
                dk_acc[j] = part_k
            else:
                dv_acc[j] += part_v
                dk_acc[j] += part_k
        dkv_tx[a, :, 0] = (dk_acc[a] * SCALE).astype(BF16).reshape(4, 128, 128)
        dkv_tx[a, :, 1] = dv_acc[a].astype(BF16).reshape(4, 128, 128)
        dq_tx[a] = (grad_q * SCALE).T.astype(BF16).reshape(4, 2, 128, 128)
        for dx, e in ((1, 0), (1, 1), (0, 1), (0, 0)):
            src = dkv_tx.at[a, dx * 2 + other(e)]
            dst = dkv_rx.at[a, dx, e]
            if dx or e:
                got_grads[a].append(send(src, dst, dev(dx=dx, dc=e)))
            else:
                kept[a].append(local(src, dst))
        for dy, e in order + [(0, 0)]:
            src = dq_tx.at[a, dy, other(e)]
            dst = dq_rx.at[a, (4 - dy) % 4, e]
            if dy or e:
                got_grads[a].append(send(src, dst, dev(dy=dy, dc=e)))
            else:
                kept[a].append(local(src, dst))
    def finish_grads(a):
        for copy in got_grads[a]:
            copy.wait_recv()
        for copy in kept[a]:
            copy.wait()
        rows = slice(a * 128, (a + 1) * 128)
        for e in range(2):
            base = pl.multiple_of(other(e) * 128, 128)
            total = sum(dq_rx[a, i, e].astype(F32) for i in range(4))
            grads[0, rows, pl.ds(base, 128)] = total.astype(BF16)
            for i in range(2):
                total = dkv_rx[a, 0, e, i].astype(F32) + dkv_rx[a, 1, e, i].astype(F32)
                grads[1 + i, rows, pl.ds(base, 128)] = total.astype(BF16)

    blocks = (2, 1, 0)
    pieces = [slice(a * 128, (a + 1) * 128) for a in blocks]

    def far(r):
        return lax.rem(z + r + 8, 8)

    def product(p, start, width):
        places = pl.ds(pl.multiple_of(start, 128), width)
        weights = (wq_v, wk_v, wv_v)
        return sum(nt(grads[i, pieces[p], :], weights[i][places, :]) for i in range(3))

    def rows_of(p, ref, *index):
        return ref.at[(*index, pieces[p], slice(None))]

    got_x = {}

    def start_x(p):
        theirs = product(p, lax.rem(xh + 1, 2) * 1024, 1024).astype(BF16)
        for i in range(8):
            x_tx[i, pieces[p], :] = theirs[:, i * 128 : (i + 1) * 128]
        mine = product(p, xh * 1024, 1024)
        for i in range(8):
            a_own[i, pieces[p], :] = mine[:, i * 128 : (i + 1) * 128]

    def more_x(p, places):
        for r in places:
            i = far(r)
            got_x[r, p] = send(rows_of(p, x_tx, i), rows_of(p, x_rx, i), dev(dh=1))

    def own_b(r, p):
        return product(p, 2048 + far(r) * 256, 256)

    used_x = set()

    def own_a(r, p):
        if (r, p) not in used_x:
            used_x.add((r, p))
            got_x[r, p].wait_recv()
        i = far(r)
        return a_own[i, pieces[p], :] + x_rx[i, pieces[p], :].astype(F32)

    class Ring:
        def __init__(self, own, tx, rx, far_way):
            self.own, self.tx, self.rx, self.far_way, self.got = own, tx, rx, far_way, {}

        def hop(self, w, step, p):
            value = self.own((4 - step) * (1 - 2 * w) if step else 4, p)
            if (w, step - 1, p) in self.got:
                self.got[w, step - 1, p].wait_recv()
                value += self.rx[w, step - 1, pieces[p], :].astype(F32)
            self.tx[w, step, pieces[p], :] = value.astype(BF16)
            self.got[w, step, p] = send(
                rows_of(p, self.tx, w, step), rows_of(p, self.rx, w, step), dev(dz=1 - 2 * w)
            )

        def wave(self, k, p):
            way = self.far_way[p]
            self.hop(way, k, p)
            if k < 3:
                self.hop(1 - way, k + 1, p)

        def last(self, p):
            value = self.own(0, p)
            for w in range(2):
                self.got[w, 3, p].wait_recv()
                value += self.rx[w, 3, pieces[p], :].astype(F32)
            return value

    ring_b = Ring(own_b, b_tx, b_rx, (0, 1, 0))
    ring_a = Ring(own_a, a_tx, a_rx, (0, 1, 1))
    stores = []
    got_swap = {}
    gather_b, gather_a = {}, {}
    got_across = {}
    own_out_a = out_a.at[xh]

    def store_b(r):
        i = far(r)
        lanes = pl.ds(pl.multiple_of(2048 + i * 256, 128), 256)
        stores.append(local(out_b.at[i], out.at[:, lanes]))

    def store_a(r, dh):
        i, h = far(r), lax.rem(xh + dh, 2)
        lanes = pl.ds(pl.multiple_of(h * 1024 + i * 128, 128), 128)
        stores.append(local(out_a.at[h, i], out.at[:, lanes]))

    def pass_on(got, buf, far_way, step, p):
        for w in range(2):
            if step and (step < 4 or far_way[p] == w):
                got[w, step - 1, p].wait_recv()
            if step < 3 or (step == 3 and far_way[p] == w):
                piece = rows_of(p, buf, far(-step * (1 - 2 * w)))
                got[w, step, p] = send(piece, piece, dev(dz=1 - 2 * w))

    def places(step):
        return [0] if step == 0 else [4] if step == 4 else [-step, step]

    def stage_b(k, p):
        if k < 4:
            ring_b.wave(k, p)
        elif k == 4:
            swap_tx[pieces[p], :] = ring_b.last(p).astype(BF16)
            got_swap[p] = send(rows_of(p, swap_tx), rows_of(p, swap_rx), dev(dh=1))
        elif k < 10:
            if k == 5:
                got_swap[p].wait_recv()
                out_b[z, pieces[p], :] = (
                    swap_tx[pieces[p], :].astype(F32) + swap_rx[pieces[p], :].astype(F32)
                ).astype(BF16)
            pass_on(gather_b, out_b, ring_b.far_way, k - 5, p)
            if p == 2:
                for r in places(k - 5):
                    store_b(r)

    def stage_a(k, p):
        if k < 4:
            ring_a.wave(k, p)
        elif k < 9:
            if k == 4:
                out_a[xh, z, pieces[p], :] = ring_a.last(p).astype(BF16)
            pass_on(gather_a, own_out_a, ring_a.far_way, k - 4, p)
            for r in places(k - 4):
                piece = rows_of(p, out_a, xh, far(r))
                got_across[r, p] = send(piece, piece, dev(dh=1))
                if p == 2:
                    store_a(r, 0)

    offset = (0, 1, 1)
    for turn in range(12):
        if turn >= 6:
            for p in (0, 1, 2):
                if turn >= offset[p] + 1:
                    stage_a(turn - offset[p] - 1, p)
        for p in (0, 1, 2):
            if turn == offset[p]:
                finish_grads(blocks[p])
            if turn >= offset[p]:
                stage_b(turn - offset[p], p)
            if turn == offset[p]:
                start_x(p)
            if 0 <= turn - offset[p] < 4:
                more_x(p, ((4, 3, -3), (2, -2), (1, -1), (0,))[turn - offset[p]])
        if turn < 6:
            for p in (0, 1, 2):
                if turn >= offset[p] + 1:
                    stage_a(turn - offset[p] - 1, p)
    for r in (0, -1, 1, -2, 2, -3, 3, 4):
        for p in range(3):
            got_across[r, p].wait_recv()
        store_a(r, 1)
    for copy in stores:
        copy.wait()
    for copy in started:
        copy.wait_send()


def shards(tokens, w_query, w_key, w_value, grad_out):
    anywhere = pl.BlockSpec(memory_space=pl.ANY)
    scratch = [
        ((ROWS, D), BF16), ((D, 256), BF16), ((D, 256), BF16), ((D, 256), BF16),
        ((2, SUB, 128, 128), BF16), ((2, SUB, 128, 128), BF16), ((2, SUB, 128, 128), BF16),
        ((SUB, 1024, 128), BF16), ((SUB, 1024, 128), BF16),
        ((SUB, 512, 128), BF16), ((SUB, 512, 128), BF16), ((SUB, 128, 512), BF16),
        ((512, 256), jnp.int32), ((6, 512, 1024), BF16), ((6, 512, 1024), BF16),
        ((SUB, 8, 1024), F32), ((SUB, 8, 1024), F32), ((SUB, 8, 1024), F32), ((8, 1024), F32), ((3, 8, 1024), F32), ((8, 1024), F32),
        ((2, 512, 1024), BF16), ((2, 512, 1024), BF16), ((SUB, 512, 128), F32), ((SUB, 512, 128), F32),
        ((SUB, 4, 2, 128, 128), BF16), ((SUB, 4, 2, 128, 128), BF16),
        ((SUB, 4, 2, 128, 128), BF16), ((SUB, 2, 2, 2, 128, 128), BF16), ((3, ROWS, 256), BF16),
        ((8, ROWS, 128), BF16), ((8, ROWS, 128), BF16), ((8, ROWS, 128), F32),
        ((2, 4, ROWS, 256), BF16), ((2, 4, ROWS, 256), BF16),
        ((2, 4, ROWS, 128), BF16), ((2, 4, ROWS, 128), BF16),
        ((ROWS, 256), BF16), ((ROWS, 256), BF16),
        ((8, ROWS, 256), BF16), ((2, 8, ROWS, 128), BF16),
    ]
    return pl.pallas_call(
        kernel,
        out_shape=pltpu.VMEM((ROWS, D), BF16),
        in_specs=[anywhere] * 5,
        out_specs=pl.BlockSpec(memory_space=pltpu.VMEM),
        scratch_shapes=[pltpu.VMEM(shape, kind) for shape, kind in scratch]
        + [
            pltpu.SemaphoreType.DMA((COPIES,)),
            pltpu.SemaphoreType.DMA((COPIES,)),
            pltpu.SemaphoreType.DMA((LOCALS,)),
        ],
        compiler_params=pltpu.CompilerParams(
            collective_id=0, has_side_effects=True, vmem_limit_bytes=54 * 2**20
        ),
    )(tokens, w_query, w_key, w_value, grad_out.reshape(SUB, 128, 256))


def solution(mesh):
    placed = (P("seq", None), P(None, "tp"), P(None, "tp"), P(None, "tp"), P("seq", "tp"))
    return jax.shard_map(
        shards, mesh=mesh, in_specs=placed, out_specs=P("seq", None), check_vma=False
    )
```
